32 devices in a mesh: seq: 16 (over z, y, x), tp: 2 (over core).
Axes of the slice: x: 2, y: 2, z: 4, core: 2. Of those that a mesh axis runs over, the one named last changes fastest.
Arguments:
- conv_in: bfloat16 [4096, 16384], P('seq', 'tp'), may hold values from -6 to 6
- gate_in: bfloat16 [4096, 16384], P('seq', 'tp'), may hold values from -6 to 6
- q_proj: bfloat16 [4096, 8192], P('seq', 'tp'), may hold values from -6 to 6
- k_proj: bfloat16 [4096, 1024], P('seq', 'tp'), may hold values from -6 to 6
- v_proj: bfloat16 [4096, 1024], P('seq', 'tp'), may hold values from -6 to 6
- conv_weight: float32 [4, 16384], P(None, 'tp'), may hold values from -3 to 3
- conv_bias: float32 [16384], P('tp'), may hold values from -0.5 to 0.5
- proj_dt_weight: bfloat16 [16384, 512], P('tp'), may hold values from -0.046875 to 0.046875
- proj_bc_weight: bfloat16 [32, 16384], P(None, 'tp'), may hold values from -0.046875 to 0.046875
- dt_gain: float32 [512], replicated, may hold values from 0.1 to 1.9
- dt_weight: bfloat16 [512, 16384], P(None, 'tp'), may hold values from -0.25 to 0.25
- dt_bias: float32 [16384], P('tp'), may hold values from -5 to -2
- decay_rate: float32 [16, 16384], P(None, 'tp'), may hold values from 1e-05 to 2
- skip_weight: float32 [16384], P('tp'), may hold values from 0.5 to 1.5
Outputs:
- mamba_out: bfloat16 [4096, 16384], P('seq', 'tp')
- attn_out: bfloat16 [4096, 8192], P('seq', 'tp')
The draws below stay inside these ranges and needn't reach their ends.
All inputs are finite; a program needn't handle non-finite values.
Results may differ from the reference program's by a relative error of at most 0.0051.
Values may be sent and summed in bfloat16 or wider, within the bound.
A program may use at most 192 MiB of HBM per device.

```python
import math
import jax
import jax.numpy as jnp
from jax import lax

E = 16384
NSTATE = 16
KCONV = 4
RANK = 512
H = 64
KVH = 8
HD = 128
TOK_DEV = 256
WINDOW = 2048
TOKENS = 4096


def draw_k_proj(key, part):
    shape_keys = (TOKENS, KVH, HD)
    values = jnp.clip(jax.random.normal(jax.random.fold_in(key, 2), shape_keys, jnp.float32), -6.0, 6.0)
    return values.reshape(TOKENS, KVH * HD).astype(jnp.bfloat16)


def draw_q_proj(key, part):
    shape_queries = (TOKENS, KVH, H // KVH, HD)
    values = jnp.clip(jax.random.normal(jax.random.fold_in(key, 1), shape_queries, jnp.float32), -6.0, 6.0)
    return values.reshape(TOKENS, H * HD).astype(jnp.bfloat16)


def level_of(own_key, extent, cuts, least, largest):
    loudness = 1.0
    for axis_at, parts in cuts:
        heights = jax.random.uniform(jax.random.fold_in(jax.random.fold_in(own_key, 6), axis_at), (parts,), jnp.float32, least / len(cuts), largest / len(cuts))
        loudness = loudness * jnp.repeat(jnp.exp(heights), extent[axis_at] // parts).reshape((-1,) + (1,) * (len(extent) - 1 - axis_at))
    return loudness


def gaussian(key, dims, deviation, limit, pieces=(), kind=jnp.bfloat16):
    gain = level_of(key, dims, pieces, -0.22, 0.18) if pieces else 1.0
    drawn = jax.random.normal(key, dims, jnp.float32) * deviation * gain
    return jnp.minimum(jnp.maximum(drawn, -limit), limit).astype(kind)


def setup_inputs(seed: int = 0) -> dict:
    seeds = jax.random.split(jax.random.key(seed), 15)
    return {
        "conv_in": gaussian(seeds[0], (TOKENS, E), 1.0, 6.0, ((0, 16), (1, 2))),
        "gate_in": gaussian(seeds[1], (TOKENS, E), 1.0, 6.0, ((0, 16), (1, 2))),
        "q_proj": draw_q_proj(jax.random.fold_in(seeds[14], 71), 0),
        "k_proj": draw_k_proj(jax.random.fold_in(seeds[14], 71), 0),
        "v_proj": gaussian(seeds[4], (TOKENS, KVH * HD), 1.0, 6.0, ((0, 16), (1, 2))),
        "conv_weight": gaussian(seeds[5], (KCONV, E), KCONV ** -0.5, 3.0, ((1, 2),), jnp.float32),
        "conv_bias": jnp.clip(jax.random.uniform(seeds[6], (E,), jnp.float32, -0.5, 0.5) * level_of(seeds[6], (E,), ((0, 2),), -0.4, 0.0), -0.5, 0.5),
        "proj_dt_weight": gaussian(seeds[7], (E, RANK), E ** -0.5, 0.046875, ((0, 2),)),
        "proj_bc_weight": gaussian(seeds[8], (2 * NSTATE, E), E ** -0.5, 0.046875, ((1, 2),)),
        "dt_gain": jnp.clip(1.0 + 0.18 * jax.random.normal(seeds[9], (RANK,), jnp.float32), 0.1, 1.9),
        "dt_weight": gaussian(seeds[10], (RANK, E), RANK ** -0.5, 0.25, ((1, 2),)),
        "dt_bias": jnp.clip(-5.0 + 3.0 * jax.random.uniform(seeds[11], (E,), jnp.float32) ** level_of(seeds[11], (E,), ((0, 2),), -0.2, 0.2), -5.0, -2.0),
        "decay_rate": jnp.clip(jnp.exp(math.log(2.0) - 12.206073 * jax.random.uniform(seeds[12], (NSTATE, E), jnp.float32) ** level_of(seeds[12], (NSTATE, E), ((1, 2),), -0.2, 0.2)), 9.999999747378752e-06, 2.0),
        "skip_weight": jnp.clip(0.5 + 1.0 * jax.random.uniform(seeds[13], (E,), jnp.float32) ** level_of(seeds[13], (E,), ((0, 2),), -0.2, 0.2), 0.5, 1.5),
    }


epsilon = 1e-06

def causal_conv(padded, conv_weight, conv_bias, length):
    summed = conv_bias[None, :] + jnp.zeros((length, padded.shape[1]), jnp.float32)
    for offset in range(KCONV):
        summed = summed + conv_weight[offset][None, :] * padded[offset:offset + length]
    return jax.nn.silu(summed).astype(jnp.bfloat16)

def rank_norm(rank_low, dt_gain):
    mean_square = lax.optimization_barrier(jnp.mean(rank_low * rank_low, axis=-1, keepdims=True))
    return (rank_low * lax.rsqrt(mean_square + epsilon) * dt_gain[None, :]).astype(jnp.bfloat16)

def mamba_part(conv_in, gate_in, conv_weight, conv_bias, proj_dt_weight, proj_bc_weight, dt_gain, dt_weight, dt_bias, decay_rate, skip_weight):
    tokens_all, channels = conv_in.shape
    block_width = min(2048, channels)
    block_count = channels // block_width

    def conv_block(index_block):
        first_col = (index_block * block_width).astype(jnp.int32)
        inputs_block = lax.dynamic_slice_in_dim(conv_in, first_col, block_width, 1).astype(jnp.float32)
        padded = jnp.concatenate([jnp.zeros((KCONV - 1, block_width), jnp.float32), inputs_block], axis=0)
        taps = lax.dynamic_slice_in_dim(conv_weight, first_col, block_width, 1)
        biases = lax.dynamic_slice_in_dim(conv_bias, first_col, block_width, 0)
        return causal_conv(padded, taps, biases, tokens_all)
    activated = lax.map(conv_block, jnp.arange(block_count, dtype=jnp.int32))

    def add_rank(index_block, carry_pair):
        rank_sum, state_sum = carry_pair
        index_now = jnp.asarray(index_block).astype(jnp.int32)
        first_col = (index_now * block_width).astype(jnp.int32)
        block_values = activated[index_now]
        rank_sum = rank_sum + jnp.dot(block_values, lax.dynamic_slice_in_dim(proj_dt_weight, first_col, block_width, 0), preferred_element_type=jnp.float32)
        state_sum = state_sum + lax.dot_general(lax.dynamic_slice_in_dim(proj_bc_weight, first_col, block_width, 1), block_values, (((1,), (1,)), ((), ())), preferred_element_type=jnp.float32)
        return (rank_sum, state_sum)
    rank_low, state_in = lax.fori_loop(0, block_count, add_rank, (jnp.zeros((tokens_all, RANK), jnp.float32), jnp.zeros((2 * NSTATE, tokens_all), jnp.float32)))
    rank_normed = rank_norm(rank_low, dt_gain)
    input_rows = state_in[:NSTATE]
    output_rows = state_in[NSTATE:]

    def scan_block(index_block):
        first_col = (index_block * block_width).astype(jnp.int32)
        block_values = activated[index_block].astype(jnp.float32)
        step_size = jax.nn.softplus(jnp.dot(rank_normed, lax.dynamic_slice_in_dim(dt_weight, first_col, block_width, 1), preferred_element_type=jnp.float32) + lax.dynamic_slice_in_dim(dt_bias, first_col, block_width, 0)[None, :])
        drive_term = step_size * block_values
        rate_block = lax.dynamic_slice_in_dim(decay_rate, first_col, block_width, 1)

        def advance(hidden_state, inputs_now):
            step_now, drive_now, input_now, output_now = inputs_now
            hidden_state = jnp.exp(-rate_block * step_now[None, :]) * hidden_state + input_now[:, None] * drive_now[None, :]
            return (hidden_state, lax.optimization_barrier(jnp.sum(output_now[:, None] * hidden_state, axis=0)))
        final_state, outputs = lax.scan(advance, jnp.zeros((NSTATE, block_width), jnp.float32), (step_size, drive_term, input_rows.T, output_rows.T))
        gate_block = lax.dynamic_slice_in_dim(gate_in, first_col, block_width, 1).astype(jnp.float32)
        skip_block = lax.dynamic_slice_in_dim(skip_weight, first_col, block_width, 0)
        return ((outputs + skip_block[None, :] * block_values) * jax.nn.silu(gate_block)).astype(jnp.bfloat16)
    mixed = lax.map(scan_block, jnp.arange(block_count, dtype=jnp.int32))
    return mixed.transpose(1, 0, 2).reshape(tokens_all, channels)

def attention_part(q_proj, k_proj, v_proj):
    tokens_all = q_proj.shape[0]
    grouping = H // KVH
    queries = q_proj.reshape(tokens_all, KVH, grouping, HD)
    keys_pad = jnp.concatenate([jnp.zeros((WINDOW, KVH * HD), k_proj.dtype), k_proj], axis=0).reshape(WINDOW + tokens_all, KVH, HD)
    values_pad = jnp.concatenate([jnp.zeros((WINDOW, KVH * HD), v_proj.dtype), v_proj], axis=0).reshape(WINDOW + tokens_all, KVH, HD)
    block_count = tokens_all // TOK_DEV

    def one_block(index_block):
        first_row = (index_block * TOK_DEV).astype(jnp.int32)
        query_block = lax.dynamic_slice_in_dim(queries, first_row, TOK_DEV, 0).astype(jnp.float32)
        key_block = lax.dynamic_slice_in_dim(keys_pad, first_row, WINDOW + TOK_DEV, 0).astype(jnp.float32)
        value_block = lax.dynamic_slice_in_dim(values_pad, first_row, WINDOW + TOK_DEV, 0).astype(jnp.float32)
        scores = jnp.einsum('tkgd,skd->kgts', query_block, key_block) * (1.0 / math.sqrt(HD))
        row_ids = jnp.arange(TOK_DEV, dtype=jnp.int32)[:, None]
        col_ids = jnp.arange(WINDOW + TOK_DEV, dtype=jnp.int32)[None, :]
        distance = WINDOW + row_ids - col_ids
        in_window = (distance >= 0) & (distance < WINDOW) & (col_ids + first_row >= WINDOW)
        row_peak = lax.optimization_barrier(jnp.max(jnp.where(in_window, scores, -jnp.inf), axis=-1, keepdims=True))
        weights = jnp.exp(jnp.where(in_window, scores - row_peak, -jnp.inf)).astype(jnp.bfloat16)
        summed = lax.optimization_barrier(jnp.sum(weights.astype(jnp.float32), axis=-1))
        weighted = jnp.einsum('kgts,skd->tkgd', weights.astype(jnp.float32), value_block)
        result = weighted / summed.transpose(2, 0, 1)[..., None]
        return result.astype(jnp.bfloat16).reshape(TOK_DEV, H * HD)
    return lax.map(one_block, jnp.arange(block_count, dtype=jnp.int32)).reshape(tokens_all, H * HD)

def reference(conv_in, gate_in, q_proj, k_proj, v_proj, conv_weight, conv_bias, proj_dt_weight, proj_bc_weight, dt_gain, dt_weight, dt_bias, decay_rate, skip_weight):
    mamba_out = mamba_part(conv_in, gate_in, conv_weight, conv_bias, proj_dt_weight, proj_bc_weight, dt_gain, dt_weight, dt_bias, decay_rate, skip_weight)
    attn_out = attention_part(q_proj, k_proj, v_proj)
    return (mamba_out, attn_out)
```

```python
import functools
import math

import jax
import jax.numpy as jnp
from jax import lax
from jax.experimental import pallas as pl
from jax.experimental.pallas import tpu as pltpu
from jax.sharding import PartitionSpec as P

KCONV = 4
HD = 128
WINDOW = 2048
LANES = 128
SUBLANES = 8
GROUP = LANES * SUBLANES
TAIL = 16
LOG2E = math.log2(math.e)
FAR = -1e30
epsilon = 1e-06


def shifted(value, axis, steps):
    count = lax.axis_size(axis)
    return lax.ppermute(value, axis, [(source, source + steps) for source in range(count - steps)])


def params(mib=56):
    return pltpu.CompilerParams(vmem_limit_bytes=mib * 1024 * 1024)


def project_kernel(rank, tail_ref, x_ref, taps_ref, bias_ref, wdt_ref, wbc_ref, act_ref, sums_ref, wide):
    tokens = x_ref.shape[0]
    wide[:TAIL] = tail_ref[...].astype(jnp.float32)
    wide[TAIL:] = x_ref[...].astype(jnp.float32)
    total = bias_ref[...] + taps_ref[0:1] * wide[pl.ds(TAIL - 3, tokens)]
    for j in range(1, KCONV):
        total = total + taps_ref[j : j + 1] * wide[pl.ds(TAIL - 3 + j, tokens)]
    act = (total / (1.0 + jnp.exp(-total))).astype(jnp.bfloat16)
    act_ref[...] = act
    low = jnp.dot(act, wdt_ref[...], preferred_element_type=jnp.float32)
    state = lax.dot_general(
        act, wbc_ref[...], (((1,), (1,)), ((), ())), preferred_element_type=jnp.float32
    )
    states = state.shape[1]

    @pl.when(pl.program_id(0) == 0)
    def _():
        sums_ref[...] = jnp.zeros_like(sums_ref)

    sums_ref[:, :rank] += low
    sums_ref[:, rank : rank + states] += state


def project(tail, conv_in, taps, bias, wdt, wbc):
    tokens, channels = conv_in.shape
    rank = wdt.shape[1]
    states = wbc.shape[0]
    blocks = channels // GROUP
    return pl.pallas_call(
        functools.partial(project_kernel, rank),
        grid=(blocks,),
        in_specs=[
            pl.BlockSpec((TAIL, GROUP), lambda i: (0, i)),
            pl.BlockSpec((tokens, GROUP), lambda i: (0, i)),
            pl.BlockSpec((KCONV, GROUP), lambda i: (0, i)),
            pl.BlockSpec((1, GROUP), lambda i: (0, i)),
            pl.BlockSpec((GROUP, rank), lambda i: (i, 0)),
            pl.BlockSpec((states, GROUP), lambda i: (0, i)),
        ],
        out_specs=[
            pl.BlockSpec((tokens, GROUP), lambda i: (0, i)),
            pl.BlockSpec((tokens, rank + LANES), lambda i: (0, 0)),
        ],
        out_shape=[
            jax.ShapeDtypeStruct((tokens, channels), jnp.bfloat16),
            jax.ShapeDtypeStruct((tokens, rank + LANES), jnp.float32),
        ],
        scratch_shapes=[pltpu.VMEM((TAIL + tokens, GROUP), jnp.float32)],
        compiler_params=params(),
        cost_estimate=pl.CostEstimate(
            flops=2 * tokens * channels * (rank + states),
            bytes_accessed=4 * tokens * channels + 2 * channels * rank,
            transcendentals=tokens * channels,
        ),
        name="conv_and_projections",
    )(tail, conv_in, taps, bias, wdt, wbc)


def scan_kernel(rank, state_count, bc_ref, low_ref, gain_ref, wdt_ref, bias_ref, act_ref, rate_ref,
                y_ref, cum_ref, final_ref, normed, steps, drives):
    tokens = act_ref.shape[0]

    @pl.when(pl.program_id(0) == 0)
    def _():
        low = low_ref[:, :rank]
        mean_square = jnp.mean(low * low, axis=-1, keepdims=True)
        normed[...] = (low * lax.rsqrt(mean_square + epsilon) * gain_ref[...]).astype(jnp.bfloat16)

    for j in range(SUBLANES):
        cols = slice(j * LANES, (j + 1) * LANES)
        raw = (
            jnp.dot(normed[...], wdt_ref[:, cols], preferred_element_type=jnp.float32)
            + bias_ref[:, cols]
        )
        step = jnp.maximum(raw, 0.0) + jnp.log1p(jnp.exp(-jnp.abs(raw)))
        steps[pl.ds(j, tokens, stride=SUBLANES), :] = step
        drives[pl.ds(j, tokens, stride=SUBLANES), :] = step * act_ref[:, cols].astype(jnp.float32)

    def advance(t, carry):
        through, hidden = carry
        rows = pl.ds(pl.multiple_of(t * SUBLANES, SUBLANES), SUBLANES)
        step, drive = steps[rows, :], drives[rows, :]
        base = t * (2 * state_count)
        out = None
        new = []
        for n in range(state_count):
            h = jnp.exp2(rate_ref[0, n] * step) * hidden[n] + bc_ref[base + n] * drive
            term = bc_ref[base + state_count + n] * h
            out = term if out is None else out + term
            new.append(h)
        through = through + step
        y_ref[0, rows, :] = out
        cum_ref[0, rows, :] = through
        return through, tuple(new)

    zero = jnp.zeros((SUBLANES, LANES), jnp.float32)
    _, hidden = lax.fori_loop(0, tokens, advance, (zero, (zero,) * state_count), unroll=4)
    for n in range(state_count):
        final_ref[0, n] = hidden[n]


def local_scan(bc, low, gain, wdt, bias, act, rates):
    tokens, channels = act.shape
    rank = gain.shape[1]
    blocks, state_count = rates.shape[:2]
    rows = tokens * SUBLANES
    return pl.pallas_call(
        functools.partial(scan_kernel, rank, state_count),
        grid=(blocks,),
        in_specs=[
            pl.BlockSpec(memory_space=pltpu.SMEM),
            pl.BlockSpec(low.shape, lambda i: (0, 0)),
            pl.BlockSpec((1, rank), lambda i: (0, 0)),
            pl.BlockSpec((rank, GROUP), lambda i: (0, i)),
            pl.BlockSpec((1, GROUP), lambda i: (0, i)),
            pl.BlockSpec((tokens, GROUP), lambda i: (0, i)),
            pl.BlockSpec((1, state_count, SUBLANES, LANES), lambda i: (i, 0, 0, 0)),
        ],
        out_specs=[
            pl.BlockSpec((1, rows, LANES), lambda i: (i, 0, 0)),
            pl.BlockSpec((1, rows, LANES), lambda i: (i, 0, 0)),
            pl.BlockSpec((1, state_count, SUBLANES, LANES), lambda i: (i, 0, 0, 0)),
        ],
        out_shape=[
            jax.ShapeDtypeStruct((blocks, rows, LANES), jnp.float32),
            jax.ShapeDtypeStruct((blocks, rows, LANES), jnp.float32),
            jax.ShapeDtypeStruct((blocks, state_count, SUBLANES, LANES), jnp.float32),
        ],
        scratch_shapes=[
            pltpu.VMEM((tokens, rank), jnp.bfloat16),
            pltpu.VMEM((rows, LANES), jnp.float32),
            pltpu.VMEM((rows, LANES), jnp.float32),
        ],
        compiler_params=params(),
        cost_estimate=pl.CostEstimate(
            flops=2 * tokens * channels * rank + 8 * tokens * channels * state_count,
            bytes_accessed=12 * tokens * channels + 2 * channels * rank,
            transcendentals=tokens * channels * state_count,
        ),
        name="local_scan",
    )(bc, low, gain, wdt, bias, act, rates)


def finish_kernel(state_count, bc_ref, y_ref, cum_ref, rate_ref, enter_ref, act_ref, gate_ref, skip_ref,
                  out_ref, mixed):
    tokens = act_ref.shape[0]

    def adjust(t, carry):
        rows = pl.ds(pl.multiple_of(t * SUBLANES, SUBLANES), SUBLANES)
        through = cum_ref[0, rows, :]
        base = t * (2 * state_count) + state_count
        total = y_ref[0, rows, :]
        for n in range(state_count):
            total = total + bc_ref[base + n] * (jnp.exp2(rate_ref[0, n] * through) * enter_ref[0, n])
        mixed[rows, :] = total
        return carry

    lax.fori_loop(0, tokens, adjust, 0, unroll=4)
    for j in range(SUBLANES):
        cols = slice(j * LANES, (j + 1) * LANES)
        gate = gate_ref[:, cols].astype(jnp.float32)
        value = mixed[pl.ds(j, tokens, stride=SUBLANES), :]
        value = value + skip_ref[:, cols] * act_ref[:, cols].astype(jnp.float32)
        out_ref[:, cols] = (value * (gate / (1.0 + jnp.exp(-gate)))).astype(jnp.bfloat16)


def finish(bc, y, cum, rates, enter, act, gate, skip):
    tokens, channels = act.shape
    blocks, state_count = rates.shape[:2]
    rows = tokens * SUBLANES
    return pl.pallas_call(
        functools.partial(finish_kernel, state_count),
        grid=(blocks,),
        in_specs=[
            pl.BlockSpec(memory_space=pltpu.SMEM),
            pl.BlockSpec((1, rows, LANES), lambda i: (i, 0, 0)),
            pl.BlockSpec((1, rows, LANES), lambda i: (i, 0, 0)),
            pl.BlockSpec((1, state_count, SUBLANES, LANES), lambda i: (i, 0, 0, 0)),
            pl.BlockSpec((1, state_count, SUBLANES, LANES), lambda i: (i, 0, 0, 0)),
            pl.BlockSpec((tokens, GROUP), lambda i: (0, i)),
            pl.BlockSpec((tokens, GROUP), lambda i: (0, i)),
            pl.BlockSpec((1, GROUP), lambda i: (0, i)),
        ],
        out_specs=pl.BlockSpec((tokens, GROUP), lambda i: (0, i)),
        out_shape=jax.ShapeDtypeStruct((tokens, channels), jnp.bfloat16),
        scratch_shapes=[pltpu.VMEM((rows, LANES), jnp.float32)],
        compiler_params=params(),
        cost_estimate=pl.CostEstimate(
            flops=6 * tokens * channels * state_count,
            bytes_accessed=14 * tokens * channels,
            transcendentals=tokens * channels * state_count,
        ),
        name="carry_and_gate",
    )(bc, y, cum, rates, enter, act, gate, skip)


def attention_kernel(span, aliased, *refs):
    position, q_ref = refs[:2]
    key_refs = refs[2 : 3 + span]
    value_refs = refs[3 + span : 4 + 2 * span]
    out_ref, keys, values, scores = refs[4 + 2 * span + aliased :]
    tokens = q_ref.shape[0]

    @pl.when(pl.program_id(0) == 0)
    def _():
        first = lax.broadcasted_iota(jnp.int32, (tokens, HD), 1) == 0
        for d in range(span + 1):
            rows = slice(d * tokens, (d + 1) * tokens)
            absent = jnp.where(position[0] >= d, 0.0, FAR)
            keys[rows, :HD] = key_refs[d][...]
            keys[rows, HD:] = jnp.where(first, absent, 0.0).astype(jnp.bfloat16)
            values[rows, :HD] = value_refs[d][...]
            values[rows, HD:] = jnp.ones((tokens, HD), jnp.bfloat16)

    ones = (lax.broadcasted_iota(jnp.int32, (tokens, HD), 1) == 0).astype(jnp.bfloat16)
    query = jnp.concatenate([q_ref[...], ones], axis=1)
    near = lax.broadcasted_iota(jnp.int32, (tokens, tokens), 1) <= lax.broadcasted_iota(
        jnp.int32, (tokens, tokens), 0
    )

    def score(d):
        return lax.dot_general(
            query,
            keys[d * tokens : (d + 1) * tokens],
            (((1,), (1,)), ((), ())),
            preferred_element_type=jnp.float32,
        )

    block = jnp.where(near, score(0), score(span))
    scores[0] = block
    peak = block
    for d in range(1, span):
        block = score(d)
        scores[d] = block
        peak = jnp.maximum(peak, block)
    factor = LOG2E / math.sqrt(HD)
    peak = jnp.max(peak, axis=-1, keepdims=True) * factor
    weight = jnp.exp2(scores[0] * factor - peak).astype(jnp.bfloat16)
    zero = jnp.zeros_like(weight)
    total = jnp.dot(
        jnp.where(near, weight, zero), values[:tokens], preferred_element_type=jnp.float32
    ) + jnp.dot(
        jnp.where(near, zero, weight), values[span * tokens :], preferred_element_type=jnp.float32
    )
    for d in range(1, span):
        weight = jnp.exp2(scores[d] * factor - peak).astype(jnp.bfloat16)
        total = total + jnp.dot(
            weight, values[d * tokens : (d + 1) * tokens], preferred_element_type=jnp.float32
        )
    out_ref[...] = (total[:, :HD] / total[:, HD:]).astype(jnp.bfloat16)


def attention(head, position, queries, pairs, before):
    tokens, width = queries.shape
    span = len(pairs) - 1
    kv_here = pairs[0].shape[1] // (2 * HD)
    grouping = width // HD // kv_here
    aliased = 0 if before is None else 1
    specs = [
        pl.BlockSpec(memory_space=pltpu.SMEM),
        pl.BlockSpec((tokens, HD), lambda i: (0, head * grouping + i)),
    ]
    specs += [pl.BlockSpec((tokens, HD), lambda i: (0, head))] * (span + 1)
    specs += [pl.BlockSpec((tokens, HD), lambda i: (0, kv_here + head))] * (span + 1)
    operands = [position, queries, *pairs, *pairs]
    if aliased:
        specs.append(pl.BlockSpec(memory_space=pl.ANY))
        operands.append(before)
    keys = tokens * (span + 1)
    return pl.pallas_call(
        functools.partial(attention_kernel, span, aliased),
        grid=(grouping,),
        in_specs=specs,
        out_specs=pl.BlockSpec((tokens, HD), lambda i: (0, head * grouping + i)),
        out_shape=jax.ShapeDtypeStruct((tokens, width), jnp.bfloat16),
        scratch_shapes=[
            pltpu.VMEM((keys, 2 * HD), jnp.bfloat16),
            pltpu.VMEM((keys, 2 * HD), jnp.bfloat16),
            pltpu.VMEM((span, tokens, tokens), jnp.float32),
        ],
        input_output_aliases={len(operands) - 1: 0} if aliased else {},
        compiler_params=params(),
        cost_estimate=pl.CostEstimate(
            flops=8 * grouping * tokens * keys * HD,
            bytes_accessed=4 * tokens * grouping * HD + 4 * keys * HD,
            transcendentals=grouping * tokens * keys,
        ),
        name="window_attention",
    )(*operands)


def per_device(
    conv_in,
    gate_in,
    q_proj,
    k_proj,
    v_proj,
    conv_weight,
    conv_bias,
    proj_dt_weight,
    proj_bc_weight,
    dt_gain,
    dt_weight,
    dt_bias,
    decay_rate,
    skip_weight,
):
    tokens, channels = conv_in.shape
    span = WINDOW // tokens
    rank = dt_gain.shape[0]
    state_count = decay_rate.shape[0]
    blocks = channels // GROUP
    kv_here = k_proj.shape[1] // HD
    seq = lax.axis_size("seq")

    tail = shifted(conv_in[tokens - (KCONV - 1) :], "seq", 1)
    tail = jnp.pad(tail, ((TAIL - (KCONV - 1), 0), (0, 0)))
    own = jnp.concatenate([k_proj, v_proj], axis=1)
    pairs = [own] + [shifted(own, "seq", d) for d in range(1, span + 1)]
    position = lax.axis_index("seq").astype(jnp.int32).reshape(1)

    act, sums = project(
        tail, conv_in, conv_weight, conv_bias[None], proj_dt_weight, proj_bc_weight
    )
    if lax.axis_size("tp") == 2:
        sums = sums + lax.ppermute(sums, "tp", [(0, 1), (1, 0)])
    else:
        sums = lax.psum(sums, "tp")
    bc = sums[:, rank : rank + 2 * state_count].reshape(-1)
    rates = (
        (decay_rate * -LOG2E).reshape(state_count, blocks, SUBLANES, LANES).transpose(1, 0, 2, 3)
    )
    y, cum, state = local_scan(bc, sums, dt_gain[None], dt_weight, dt_bias[None], act, rates)
    span_time = cum[:, -SUBLANES:, :][:, None]

    def after(earlier, later):
        time_a, state_a = earlier
        time_b, state_b = later
        return time_a + time_b, jnp.exp2(rates * time_b) * state_a + state_b

    def fetch(value, steps):
        time, held = value
        time, held = shifted((time, held.astype(jnp.bfloat16)), "seq", steps)
        return time, held.astype(jnp.float32)

    value = (span_time, state)
    value = after(fetch(value, 2), fetch(value, 1))
    reach = 2
    while reach < seq - 1:
        value = after(fetch(value, reach), value)
        reach *= 2
    enter = value[1]

    attn_out = None
    for head in range(kv_here):
        attn_out = attention(head, position, q_proj, pairs, attn_out)
    mamba_out = finish(bc, y, cum, rates, enter, act, gate_in, skip_weight[None])
    return (mamba_out, attn_out)


def solution(mesh):
    return jax.shard_map(
        per_device,
        mesh=mesh,
        in_specs=(
            P("seq", "tp"),
            P("seq", "tp"),
            P("seq", "tp"),
            P("seq", "tp"),
            P("seq", "tp"),
            P(None, "tp"),
            P("tp"),
            P("tp", None),
            P(None, "tp"),
            P(),
            P(None, "tp"),
            P("tp"),
            P(None, "tp"),
            P("tp"),
        ),
        out_specs=(P("seq", "tp"), P("seq", "tp")),
        check_vma=False,
    )
```

```python
import functools
import math

import jax
import jax.numpy as jnp
from jax import lax
from jax.experimental import pallas as pl
from jax.experimental.pallas import tpu as pltpu
from jax.sharding import PartitionSpec as P

KCONV = 4
HD = 128
WINDOW = 2048
LANES = 128
SUBLANES = 8
GROUP = LANES * SUBLANES
TAIL = 16
LOG2E = math.log2(math.e)
FAR = -1e30
epsilon = 1e-06


def shifted(value, axis, steps):
    count = lax.axis_size(axis)
    return lax.ppermute(value, axis, [(source, source + steps) for source in range(count - steps)])


def params(mib=56):
    return pltpu.CompilerParams(vmem_limit_bytes=mib * 1024 * 1024)


def project_kernel(rank, tail_ref, x_ref, taps_ref, bias_ref, wdt_ref, wbc_ref, act_ref, sums_ref, wide):
    tokens = x_ref.shape[0]
    wide[:TAIL] = tail_ref[...].astype(jnp.float32)
    wide[TAIL:] = x_ref[...].astype(jnp.float32)
    total = bias_ref[...] + taps_ref[0:1] * wide[pl.ds(TAIL - 3, tokens)]
    for j in range(1, KCONV):
        total = total + taps_ref[j : j + 1] * wide[pl.ds(TAIL - 3 + j, tokens)]
    act = (total / (1.0 + jnp.exp(-total))).astype(jnp.bfloat16)
    act_ref[...] = act
    low = jnp.dot(act, wdt_ref[...], preferred_element_type=jnp.float32)
    state = lax.dot_general(
        act, wbc_ref[...], (((1,), (1,)), ((), ())), preferred_element_type=jnp.float32
    )
    states = state.shape[1]

    @pl.when(pl.program_id(0) == 0)
    def _():
        sums_ref[...] = jnp.zeros_like(sums_ref)

    sums_ref[:, :rank] += low
    sums_ref[:, rank : rank + states] += state


def project(tail, conv_in, taps, bias, wdt, wbc):
    tokens, channels = conv_in.shape
    rank = wdt.shape[1]
    states = wbc.shape[0]
    blocks = channels // GROUP
    return pl.pallas_call(
        functools.partial(project_kernel, rank),
        grid=(blocks,),
        in_specs=[
            pl.BlockSpec((TAIL, GROUP), lambda i: (0, i)),
            pl.BlockSpec((tokens, GROUP), lambda i: (0, i)),
            pl.BlockSpec((KCONV, GROUP), lambda i: (0, i)),
            pl.BlockSpec((1, GROUP), lambda i: (0, i)),
            pl.BlockSpec((GROUP, rank), lambda i: (i, 0)),
            pl.BlockSpec((states, GROUP), lambda i: (0, i)),
        ],
        out_specs=[
            pl.BlockSpec((tokens, GROUP), lambda i: (0, i)),
            pl.BlockSpec((tokens, rank + LANES), lambda i: (0, 0)),
        ],
        out_shape=[
            jax.ShapeDtypeStruct((tokens, channels), jnp.bfloat16),
            jax.ShapeDtypeStruct((tokens, rank + LANES), jnp.float32),
        ],
        scratch_shapes=[pltpu.VMEM((TAIL + tokens, GROUP), jnp.float32)],
        compiler_params=params(),
        cost_estimate=pl.CostEstimate(
            flops=2 * tokens * channels * (rank + states),
            bytes_accessed=4 * tokens * channels + 2 * channels * rank,
            transcendentals=tokens * channels,
        ),
        name="conv_and_projections",
    )(tail, conv_in, taps, bias, wdt, wbc)


def scan_kernel(rank, state_count, bc_ref, low_ref, gain_ref, wdt_ref, bias_ref, act_ref, rate_ref,
                y_ref, cum_ref, packed_ref, normed, steps, drives):
    tokens = act_ref.shape[0]
    pair = rate_ref.shape[0]

    @pl.when(pl.program_id(0) == 0)
    def _():
        low = low_ref[:, :rank]
        mean_square = jnp.mean(low * low, axis=-1, keepdims=True)
        normed[...] = (low * lax.rsqrt(mean_square + epsilon) * gain_ref[...]).astype(jnp.bfloat16)

    for j in range(pair * SUBLANES):
        cols = slice(j * LANES, (j + 1) * LANES)
        where = pl.ds(j % SUBLANES, tokens, stride=SUBLANES)
        raw = (
            jnp.dot(normed[...], wdt_ref[:, cols], preferred_element_type=jnp.float32)
            + bias_ref[:, cols]
        )
        step = jnp.maximum(raw, 0.0) + jnp.log1p(jnp.exp(-jnp.abs(raw)))
        steps[j // SUBLANES, where, :] = step
        drives[j // SUBLANES, where, :] = step * act_ref[:, cols].astype(jnp.float32)

    def advance(t, carry):
        through, hidden = carry
        rows = pl.ds(pl.multiple_of(t * SUBLANES, SUBLANES), SUBLANES)
        step = [steps[p, rows, :] for p in range(pair)]
        drive = [drives[p, rows, :] for p in range(pair)]
        base = t * (2 * state_count)
        out = [None] * pair
        new = []
        for n in range(state_count):
            into, onto = bc_ref[base + n], bc_ref[base + state_count + n]
            for p in range(pair):
                h = jnp.exp2(rate_ref[p, n] * step[p]) * hidden[n * pair + p] + into * drive[p]
                out[p] = onto * h if n == 0 else out[p] + onto * h
                new.append(h)
        through = tuple(through[p] + step[p] for p in range(pair))
        for p in range(pair):
            y_ref[p, rows, :] = out[p]
            cum_ref[p, rows, :] = through[p]
        return through, tuple(new)

    zero = jnp.zeros((SUBLANES, LANES), jnp.float32)
    through, hidden = lax.fori_loop(
        0, tokens, advance, ((zero,) * pair, (zero,) * (state_count * pair)), unroll=2
    )
    size = 2 * SUBLANES
    for p in range(pair):
        for n in range(0, state_count, 2):
            both = jnp.concatenate([hidden[n * pair + p], hidden[(n + 1) * pair + p]], axis=0)
            packed_ref[p, n // 2 * size : (n // 2 + 1) * size] = both.astype(jnp.bfloat16)
        high = through[p].astype(jnp.bfloat16).astype(jnp.float32)
        middle = (through[p] - high).astype(jnp.bfloat16).astype(jnp.float32)
        low = through[p] - high - middle
        first = state_count // 2 * size
        packed_ref[p, first : first + size] = jnp.concatenate([high, middle], axis=0).astype(
            jnp.bfloat16
        )
        packed_ref[p, first + size : first + 2 * size] = jnp.concatenate([low, zero], axis=0).astype(
            jnp.bfloat16
        )


def local_scan(bc, low, gain, wdt, bias, act, rates):
    tokens, channels = act.shape
    rank = gain.shape[1]
    blocks, state_count = rates.shape[:2]
    rows = tokens * SUBLANES
    pair = 2 if blocks % 2 == 0 else 1
    width = pair * GROUP
    packed = (state_count + 4) * SUBLANES
    return pl.pallas_call(
        functools.partial(scan_kernel, rank, state_count),
        grid=(blocks // pair,),
        in_specs=[
            pl.BlockSpec(memory_space=pltpu.SMEM),
            pl.BlockSpec(low.shape, lambda i: (0, 0)),
            pl.BlockSpec((1, rank), lambda i: (0, 0)),
            pl.BlockSpec((rank, width), lambda i: (0, i)),
            pl.BlockSpec((1, width), lambda i: (0, i)),
            pl.BlockSpec((tokens, width), lambda i: (0, i)),
            pl.BlockSpec((pair, state_count, SUBLANES, LANES), lambda i: (i, 0, 0, 0)),
        ],
        out_specs=[
            pl.BlockSpec((pair, rows, LANES), lambda i: (i, 0, 0)),
            pl.BlockSpec((pair, rows, LANES), lambda i: (i, 0, 0)),
            pl.BlockSpec((pair, packed, LANES), lambda i: (i, 0, 0)),
        ],
        out_shape=[
            jax.ShapeDtypeStruct((blocks, rows, LANES), jnp.float32),
            jax.ShapeDtypeStruct((blocks, rows, LANES), jnp.float32),
            jax.ShapeDtypeStruct((blocks, packed, LANES), jnp.bfloat16),
        ],
        scratch_shapes=[
            pltpu.VMEM((tokens, rank), jnp.bfloat16),
            pltpu.VMEM((pair, rows, LANES), jnp.float32),
            pltpu.VMEM((pair, rows, LANES), jnp.float32),
        ],
        compiler_params=params(),
        cost_estimate=pl.CostEstimate(
            flops=2 * tokens * channels * rank + 8 * tokens * channels * state_count,
            bytes_accessed=12 * tokens * channels + 2 * channels * rank,
            transcendentals=tokens * channels * state_count,
        ),
        name="local_scan",
    )(bc, low, gain, wdt, bias, act, rates)


TOKENS_AT_ONCE = 4


def finish_kernel(state_count, position, bc_ref, y_ref, cum_ref, rate_ref, all_ref, act_ref, gate_ref,
                  skip_ref, out_ref, mixed, enter):
    tokens = act_ref.shape[0]
    pair = rate_ref.shape[0]
    size = 2 * SUBLANES
    halves = state_count // 2
    for p in range(pair):

        def compose(k, held):
            parts = all_ref[k, p, halves * size : (halves + 2) * size].astype(jnp.float32)
            span = (
                parts[:SUBLANES]
                + parts[SUBLANES : 2 * SUBLANES]
                + parts[2 * SUBLANES : 3 * SUBLANES]
            )
            new = []
            for n in range(state_count):
                if n % 2 == 0:
                    both = all_ref[k, p, n // 2 * size : (n // 2 + 1) * size].astype(jnp.float32)
                own = both[n % 2 * SUBLANES : (n % 2 + 1) * SUBLANES]
                new.append(jnp.exp2(rate_ref[p, n] * span) * held[n] + own)
            return tuple(new)

        zero = jnp.zeros((SUBLANES, LANES), jnp.float32)
        held = lax.fori_loop(0, position[0], compose, (zero,) * state_count)
        for n in range(state_count):
            enter[p, n] = held[n]

    def adjust(step, carry):
        first = step * TOKENS_AT_ONCE
        rows = [
            pl.ds(pl.multiple_of((first + u) * SUBLANES, SUBLANES), SUBLANES)
            for u in range(TOKENS_AT_ONCE)
        ]
        through = [[cum_ref[p, r, :] for r in rows] for p in range(pair)]
        total = [[y_ref[p, r, :] for r in rows] for p in range(pair)]
        base = first * (2 * state_count) + state_count
        for n in range(state_count):
            onto = [bc_ref[base + u * (2 * state_count) + n] for u in range(TOKENS_AT_ONCE)]
            for p in range(pair):
                rate, held = rate_ref[p, n], enter[p, n]
                for u in range(TOKENS_AT_ONCE):
                    total[p][u] = total[p][u] + onto[u] * (jnp.exp2(rate * through[p][u]) * held)
        for p in range(pair):
            for u in range(TOKENS_AT_ONCE):
                mixed[p, rows[u], :] = total[p][u]
        return carry

    lax.fori_loop(0, tokens // TOKENS_AT_ONCE, adjust, 0)
    for j in range(pair * SUBLANES):
        cols = slice(j * LANES, (j + 1) * LANES)
        gate = gate_ref[:, cols].astype(jnp.float32)
        value = mixed[j // SUBLANES, pl.ds(j % SUBLANES, tokens, stride=SUBLANES), :]
        value = value + skip_ref[:, cols] * act_ref[:, cols].astype(jnp.float32)
        out_ref[:, cols] = (value * (gate / (1.0 + jnp.exp(-gate)))).astype(jnp.bfloat16)


def finish(position, bc, y, cum, rates, everything, act, gate, skip):
    tokens, channels = act.shape
    blocks, state_count = rates.shape[:2]
    rows = tokens * SUBLANES
    pair = 2 if blocks % 2 == 0 else 1
    width = pair * GROUP
    peers, _, packed, _ = everything.shape
    return pl.pallas_call(
        functools.partial(finish_kernel, state_count),
        grid=(blocks // pair,),
        in_specs=[
            pl.BlockSpec(memory_space=pltpu.SMEM),
            pl.BlockSpec(memory_space=pltpu.SMEM),
            pl.BlockSpec((pair, rows, LANES), lambda i: (i, 0, 0)),
            pl.BlockSpec((pair, rows, LANES), lambda i: (i, 0, 0)),
            pl.BlockSpec((pair, state_count, SUBLANES, LANES), lambda i: (i, 0, 0, 0)),
            pl.BlockSpec((peers, pair, packed, LANES), lambda i: (0, i, 0, 0)),
            pl.BlockSpec((tokens, width), lambda i: (0, i)),
            pl.BlockSpec((tokens, width), lambda i: (0, i)),
            pl.BlockSpec((1, width), lambda i: (0, i)),
        ],
        out_specs=pl.BlockSpec((tokens, width), lambda i: (0, i)),
        out_shape=jax.ShapeDtypeStruct((tokens, channels), jnp.bfloat16),
        scratch_shapes=[
            pltpu.VMEM((pair, rows, LANES), jnp.float32),
            pltpu.VMEM((pair, state_count, SUBLANES, LANES), jnp.float32),
        ],
        compiler_params=params(),
        cost_estimate=pl.CostEstimate(
            flops=6 * tokens * channels * state_count,
            bytes_accessed=14 * tokens * channels,
            transcendentals=tokens * channels * state_count,
        ),
        name="carry_and_gate",
    )(position, bc, y, cum, rates, everything, act, gate, skip)


def attention_kernel(span, position, q_ref, *refs):
    key_refs = refs[: 1 + span]
    value_refs = refs[1 + span : 2 + 2 * span]
    out_ref, keys, values, scores = refs[2 + 2 * span :]
    tokens = q_ref.shape[0]

    @pl.when(pl.program_id(1) == 0)
    def _():
        first = lax.broadcasted_iota(jnp.int32, (tokens, HD), 1) == 0
        for d in range(span + 1):
            rows = slice(d * tokens, (d + 1) * tokens)
            absent = jnp.where(position[0] >= d, 0.0, FAR)
            keys[rows, :HD] = key_refs[d][0]
            keys[rows, HD:] = jnp.where(first, absent, 0.0).astype(jnp.bfloat16)
            values[rows, :HD] = value_refs[d][0]
            values[rows, HD:] = jnp.ones((tokens, HD), jnp.bfloat16)

    ones = (lax.broadcasted_iota(jnp.int32, (tokens, HD), 1) == 0).astype(jnp.bfloat16)
    query = jnp.concatenate([q_ref[...], ones], axis=1)
    near = lax.broadcasted_iota(jnp.int32, (tokens, tokens), 1) <= lax.broadcasted_iota(
        jnp.int32, (tokens, tokens), 0
    )

    def score(d):
        return lax.dot_general(
            query,
            keys[d * tokens : (d + 1) * tokens],
            (((1,), (1,)), ((), ())),
            preferred_element_type=jnp.float32,
        )

    block = jnp.where(near, score(0), score(span))
    scores[0] = block
    peak = block
    for d in range(1, span):
        block = score(d)
        scores[d] = block
        peak = jnp.maximum(peak, block)
    factor = LOG2E / math.sqrt(HD)
    peak = jnp.max(peak, axis=-1, keepdims=True) * factor
    weight = jnp.exp2(scores[0] * factor - peak).astype(jnp.bfloat16)
    zero = jnp.zeros_like(weight)
    total = jnp.dot(
        jnp.where(near, weight, zero), values[:tokens], preferred_element_type=jnp.float32
    ) + jnp.dot(
        jnp.where(near, zero, weight), values[span * tokens :], preferred_element_type=jnp.float32
    )
    for d in range(1, span):
        weight = jnp.exp2(scores[d] * factor - peak).astype(jnp.bfloat16)
        total = total + jnp.dot(
            weight, values[d * tokens : (d + 1) * tokens], preferred_element_type=jnp.float32
        )
    out_ref[...] = (total[:, :HD] / total[:, HD:]).astype(jnp.bfloat16)


def attention(position, queries, pairs, span):
    tokens, width = queries.shape
    kv_here = pairs.shape[2] // (2 * HD)
    grouping = width // HD // kv_here
    keys = tokens * (span + 1)

    def block(distance, offset):
        return pl.BlockSpec(
            (1, tokens, HD),
            lambda h, i, at: (jnp.maximum(at[0] - distance, 0), 0, offset + h),
        )

    specs = [pl.BlockSpec((tokens, HD), lambda h, i, at: (0, h * grouping + i))]
    specs += [block(d, 0) for d in range(span + 1)]
    specs += [block(d, kv_here) for d in range(span + 1)]
    return pl.pallas_call(
        functools.partial(attention_kernel, span),
        grid_spec=pltpu.PrefetchScalarGridSpec(
            num_scalar_prefetch=1,
            grid=(kv_here, grouping),
            in_specs=specs,
            out_specs=pl.BlockSpec((tokens, HD), lambda h, i, at: (0, h * grouping + i)),
            scratch_shapes=[
                pltpu.VMEM((keys, 2 * HD), jnp.bfloat16),
                pltpu.VMEM((keys, 2 * HD), jnp.bfloat16),
                pltpu.VMEM((span, tokens, tokens), jnp.float32),
            ],
        ),
        out_shape=jax.ShapeDtypeStruct((tokens, width), jnp.bfloat16),
        compiler_params=params(),
        cost_estimate=pl.CostEstimate(
            flops=8 * width * tokens * keys,
            bytes_accessed=4 * tokens * width + 4 * keys * HD * kv_here,
            transcendentals=width // HD * tokens * keys,
        ),
        name="window_attention",
    )(position, queries, *([pairs] * (2 * span + 2)))


def per_device(
    conv_in,
    gate_in,
    q_proj,
    k_proj,
    v_proj,
    conv_weight,
    conv_bias,
    proj_dt_weight,
    proj_bc_weight,
    dt_gain,
    dt_weight,
    dt_bias,
    decay_rate,
    skip_weight,
):
    tokens, channels = conv_in.shape
    span = WINDOW // tokens
    rank = dt_gain.shape[0]
    state_count = decay_rate.shape[0]
    blocks = channels // GROUP

    tail = shifted(conv_in[tokens - (KCONV - 1) :], "seq", 1)
    tail = jnp.pad(tail, ((TAIL - (KCONV - 1), 0), (0, 0)))
    pairs = lax.all_gather(jnp.concatenate([k_proj, v_proj], axis=1), "seq")
    position = lax.axis_index("seq").astype(jnp.int32).reshape(1)

    act, sums = project(
        tail, conv_in, conv_weight, conv_bias[None], proj_dt_weight, proj_bc_weight
    )
    if lax.axis_size("tp") == 2:
        sums = sums + lax.ppermute(sums, "tp", [(0, 1), (1, 0)])
    else:
        sums = lax.psum(sums, "tp")
    bc = sums[:, rank : rank + 2 * state_count].reshape(-1)
    rates = (
        (decay_rate * -LOG2E).reshape(state_count, blocks, SUBLANES, LANES).transpose(1, 0, 2, 3)
    )
    y, cum, packed = local_scan(bc, sums, dt_gain[None], dt_weight, dt_bias[None], act, rates)
    everything = lax.all_gather(packed, "seq")
    attn_at, _ = lax.optimization_barrier((position, packed))
    attn_out = attention(attn_at, q_proj, pairs, span)
    finish_at, attn_out = lax.optimization_barrier((position, attn_out))
    mamba_out = finish(
        finish_at, bc, y, cum, rates, everything, act, gate_in, skip_weight[None]
    )
    return (mamba_out, attn_out)


def solution(mesh):
    return jax.shard_map(
        per_device,
        mesh=mesh,
        in_specs=(
            P("seq", "tp"),
            P("seq", "tp"),
            P("seq", "tp"),
            P("seq", "tp"),
            P("seq", "tp"),
            P(None, "tp"),
            P("tp"),
            P("tp", None),
            P(None, "tp"),
            P(),
            P(None, "tp"),
            P("tp"),
            P(None, "tp"),
            P("tp"),
        ),
        out_specs=(P("seq", "tp"), P("seq", "tp")),
        check_vma=False,
    )
```

```python
import functools
import math

import jax
import jax.numpy as jnp
from jax import lax
from jax.experimental import pallas as pl
from jax.experimental.pallas import tpu as pltpu
from jax.sharding import PartitionSpec as P

KCONV = 4
HD = 128
WINDOW = 2048
LANES = 128
SUBLANES = 8
GROUP = LANES * SUBLANES
TAIL = 16
LOG2E = math.log2(math.e)
FAR = -1e30
epsilon = 1e-06


def shifted(value, axis, steps):
    count = lax.axis_size(axis)
    return lax.ppermute(value, axis, [(source, source + steps) for source in range(count - steps)])


def params(mib=56):
    return pltpu.CompilerParams(vmem_limit_bytes=mib * 1024 * 1024)


def project_kernel(rank, tail_ref, x_ref, taps_ref, bias_ref, wdt_ref, wbc_ref, act_ref, sums_ref, wide):
    tokens = x_ref.shape[0]
    wide[:TAIL] = tail_ref[...].astype(jnp.float32)
    wide[TAIL:] = x_ref[...].astype(jnp.float32)
    total = bias_ref[...] + taps_ref[0:1] * wide[pl.ds(TAIL - 3, tokens)]
    for j in range(1, KCONV):
        total = total + taps_ref[j : j + 1] * wide[pl.ds(TAIL - 3 + j, tokens)]
    act = (total / (1.0 + jnp.exp(-total))).astype(jnp.bfloat16)
    act_ref[...] = act
    low = jnp.dot(act, wdt_ref[...], preferred_element_type=jnp.float32)
    state = lax.dot_general(
        act, wbc_ref[...], (((1,), (1,)), ((), ())), preferred_element_type=jnp.float32
    )
    states = state.shape[1]

    @pl.when(pl.program_id(0) == 0)
    def _():
        sums_ref[...] = jnp.zeros_like(sums_ref)

    sums_ref[:, :rank] += low
    sums_ref[:, rank : rank + states] += state


def project(tail, conv_in, taps, bias, wdt, wbc):
    tokens, channels = conv_in.shape
    rank = wdt.shape[1]
    states = wbc.shape[0]
    blocks = channels // GROUP
    return pl.pallas_call(
        functools.partial(project_kernel, rank),
        grid=(blocks,),
        in_specs=[
            pl.BlockSpec((TAIL, GROUP), lambda i: (0, i)),
            pl.BlockSpec((tokens, GROUP), lambda i: (0, i)),
            pl.BlockSpec((KCONV, GROUP), lambda i: (0, i)),
            pl.BlockSpec((1, GROUP), lambda i: (0, i)),
            pl.BlockSpec((GROUP, rank), lambda i: (i, 0)),
            pl.BlockSpec((states, GROUP), lambda i: (0, i)),
        ],
        out_specs=[
            pl.BlockSpec((tokens, GROUP), lambda i: (0, i)),
            pl.BlockSpec((tokens, rank + LANES), lambda i: (0, 0)),
        ],
        out_shape=[
            jax.ShapeDtypeStruct((tokens, channels), jnp.bfloat16),
            jax.ShapeDtypeStruct((tokens, rank + LANES), jnp.float32),
        ],
        scratch_shapes=[pltpu.VMEM((TAIL + tokens, GROUP), jnp.float32)],
        compiler_params=params(),
        cost_estimate=pl.CostEstimate(
            flops=2 * tokens * channels * (rank + states),
            bytes_accessed=4 * tokens * channels + 2 * channels * rank,
            transcendentals=tokens * channels,
        ),
        name="conv_and_projections",
    )(tail, conv_in, taps, bias, wdt, wbc)


def scan_kernel(rank, state_count, bc_ref, low_ref, gain_ref, wdt_ref, bias_ref, act_ref, rate_ref,
                y_ref, cum_ref, packed_ref, normed, steps, drives):
    tokens = act_ref.shape[0]
    pair = rate_ref.shape[0]

    @pl.when(pl.program_id(0) == 0)
    def _():
        low = low_ref[:, :rank]
        mean_square = jnp.mean(low * low, axis=-1, keepdims=True)
        normed[...] = (low * lax.rsqrt(mean_square + epsilon) * gain_ref[...]).astype(jnp.bfloat16)

    for j in range(pair * SUBLANES):
        cols = slice(j * LANES, (j + 1) * LANES)
        where = pl.ds(j % SUBLANES, tokens, stride=SUBLANES)
        raw = (
            jnp.dot(normed[...], wdt_ref[:, cols], preferred_element_type=jnp.float32)
            + bias_ref[:, cols]
        )
        step = jnp.maximum(raw, 0.0) + jnp.log1p(jnp.exp(-jnp.abs(raw)))
        steps[j // SUBLANES, where, :] = step
        drives[j // SUBLANES, where, :] = step * act_ref[:, cols].astype(jnp.float32)

    def advance(t, carry):
        through, hidden = carry
        rows = pl.ds(pl.multiple_of(t * SUBLANES, SUBLANES), SUBLANES)
        step = [steps[p, rows, :] for p in range(pair)]
        drive = [drives[p, rows, :] for p in range(pair)]
        base = t * (2 * state_count)
        out = [None] * pair
        new = []
        for n in range(state_count):
            into, onto = bc_ref[base + n], bc_ref[base + state_count + n]
            for p in range(pair):
                h = jnp.exp2(rate_ref[p, n] * step[p]) * hidden[n * pair + p] + into * drive[p]
                out[p] = onto * h if n == 0 else out[p] + onto * h
                new.append(h)
        through = tuple(through[p] + step[p] for p in range(pair))
        for p in range(pair):
            y_ref[p, rows, :] = out[p]
            cum_ref[p, rows, :] = through[p]
        return through, tuple(new)

    zero = jnp.zeros((SUBLANES, LANES), jnp.float32)
    through, hidden = lax.fori_loop(
        0, tokens, advance, ((zero,) * pair, (zero,) * (state_count * pair)), unroll=4
    )
    size = 2 * SUBLANES
    for p in range(pair):
        for n in range(0, state_count, 2):
            both = jnp.concatenate([hidden[n * pair + p], hidden[(n + 1) * pair + p]], axis=0)
            packed_ref[p, n // 2 * size : (n // 2 + 1) * size] = both.astype(jnp.bfloat16)
        high = through[p].astype(jnp.bfloat16).astype(jnp.float32)
        middle = (through[p] - high).astype(jnp.bfloat16).astype(jnp.float32)
        low = through[p] - high - middle
        first = state_count // 2 * size
        packed_ref[p, first : first + size] = jnp.concatenate([high, middle], axis=0).astype(
            jnp.bfloat16
        )
        packed_ref[p, first + size : first + 2 * size] = jnp.concatenate([low, zero], axis=0).astype(
            jnp.bfloat16
        )


def local_scan(bc, low, gain, wdt, bias, act, rates):
    tokens, channels = act.shape
    rank = gain.shape[1]
    blocks, state_count = rates.shape[:2]
    rows = tokens * SUBLANES
    pair = 1
    width = pair * GROUP
    packed = (state_count + 4) * SUBLANES
    return pl.pallas_call(
        functools.partial(scan_kernel, rank, state_count),
        grid=(blocks // pair,),
        in_specs=[
            pl.BlockSpec(memory_space=pltpu.SMEM),
            pl.BlockSpec(low.shape, lambda i: (0, 0)),
            pl.BlockSpec((1, rank), lambda i: (0, 0)),
            pl.BlockSpec((rank, width), lambda i: (0, i)),
            pl.BlockSpec((1, width), lambda i: (0, i)),
            pl.BlockSpec((tokens, width), lambda i: (0, i)),
            pl.BlockSpec((pair, state_count, SUBLANES, LANES), lambda i: (i, 0, 0, 0)),
        ],
        out_specs=[
            pl.BlockSpec((pair, rows, LANES), lambda i: (i, 0, 0)),
            pl.BlockSpec((pair, rows, LANES), lambda i: (i, 0, 0)),
            pl.BlockSpec((pair, packed, LANES), lambda i: (i, 0, 0)),
        ],
        out_shape=[
            jax.ShapeDtypeStruct((blocks, rows, LANES), jnp.float32),
            jax.ShapeDtypeStruct((blocks, rows, LANES), jnp.float32),
            jax.ShapeDtypeStruct((blocks, packed, LANES), jnp.bfloat16),
        ],
        scratch_shapes=[
            pltpu.VMEM((tokens, rank), jnp.bfloat16),
            pltpu.VMEM((pair, rows, LANES), jnp.float32),
            pltpu.VMEM((pair, rows, LANES), jnp.float32),
        ],
        compiler_params=params(),
        cost_estimate=pl.CostEstimate(
            flops=2 * tokens * channels * rank + 8 * tokens * channels * state_count,
            bytes_accessed=12 * tokens * channels + 2 * channels * rank,
            transcendentals=tokens * channels * state_count,
        ),
        name="local_scan",
    )(bc, low, gain, wdt, bias, act, rates)


def join_kernel(state_count, rate_ref, first_ref, second_ref, out_ref):
    size = 2 * SUBLANES
    mark = state_count // 2 * size

    def elapsed(ref):
        parts = ref[0, mark : mark + 2 * size].astype(jnp.float32)
        return parts[:SUBLANES] + parts[SUBLANES:size] + parts[size : size + SUBLANES]

    later = elapsed(second_ref)
    total = elapsed(first_ref) + later
    for n in range(0, state_count, 2):
        rows = slice(n // 2 * size, (n // 2 + 1) * size)
        rate = jnp.concatenate([rate_ref[0, n], rate_ref[0, n + 1]], axis=0)
        both = jnp.concatenate([later, later], axis=0)
        joined = jnp.exp2(rate * both) * first_ref[0, rows].astype(jnp.float32)
        out_ref[0, rows] = (joined + second_ref[0, rows].astype(jnp.float32)).astype(jnp.bfloat16)
    high = total.astype(jnp.bfloat16).astype(jnp.float32)
    middle = (total - high).astype(jnp.bfloat16).astype(jnp.float32)
    low = total - high - middle
    out_ref[0, mark : mark + size] = jnp.concatenate([high, middle], axis=0).astype(jnp.bfloat16)
    out_ref[0, mark + size : mark + 2 * size] = jnp.concatenate(
        [low, jnp.zeros_like(low)], axis=0
    ).astype(jnp.bfloat16)


def join(rates, first, second):
    blocks, packed, _ = first.shape
    state_count = rates.shape[1]
    part = pl.BlockSpec((1, packed, LANES), lambda i: (i, 0, 0))
    return pl.pallas_call(
        functools.partial(join_kernel, state_count),
        grid=(blocks,),
        in_specs=[
            pl.BlockSpec((1, state_count, SUBLANES, LANES), lambda i: (i, 0, 0, 0)),
            part,
            part,
        ],
        out_specs=part,
        out_shape=jax.ShapeDtypeStruct(first.shape, jnp.bfloat16),
        compiler_params=params(),
        name="join_states",
    )(rates, first, second)


TOKENS_AT_ONCE = 4


def finish_kernel(state_count, count, bc_ref, y_ref, cum_ref, rate_ref, all_ref, act_ref, gate_ref,
                  skip_ref, out_ref, mixed, enter):
    tokens = act_ref.shape[0]
    pair = rate_ref.shape[0]
    size = 2 * SUBLANES
    halves = state_count // 2
    for p in range(pair):

        def compose(k, held):
            parts = all_ref[k, p, halves * size : (halves + 2) * size].astype(jnp.float32)
            span = (
                parts[:SUBLANES]
                + parts[SUBLANES : 2 * SUBLANES]
                + parts[2 * SUBLANES : 3 * SUBLANES]
            )
            new = []
            for n in range(state_count):
                if n % 2 == 0:
                    both = all_ref[k, p, n // 2 * size : (n // 2 + 1) * size].astype(jnp.float32)
                own = both[n % 2 * SUBLANES : (n % 2 + 1) * SUBLANES]
                new.append(jnp.exp2(rate_ref[p, n] * span) * held[n] + own)
            return tuple(new)

        zero = jnp.zeros((SUBLANES, LANES), jnp.float32)
        held = lax.fori_loop(0, count[0], compose, (zero,) * state_count)
        for n in range(state_count):
            enter[p, n] = held[n]

    def adjust(step, carry):
        first = step * TOKENS_AT_ONCE
        rows = [
            pl.ds(pl.multiple_of((first + u) * SUBLANES, SUBLANES), SUBLANES)
            for u in range(TOKENS_AT_ONCE)
        ]
        through = [[cum_ref[p, r, :] for r in rows] for p in range(pair)]
        total = [[y_ref[p, r, :] for r in rows] for p in range(pair)]
        base = first * (2 * state_count) + state_count
        for n in range(state_count):
            onto = [bc_ref[base + u * (2 * state_count) + n] for u in range(TOKENS_AT_ONCE)]
            for p in range(pair):
                rate, held = rate_ref[p, n], enter[p, n]
                for u in range(TOKENS_AT_ONCE):
                    total[p][u] = total[p][u] + onto[u] * (jnp.exp2(rate * through[p][u]) * held)
        for p in range(pair):
            for u in range(TOKENS_AT_ONCE):
                mixed[p, rows[u], :] = total[p][u]
        return carry

    lax.fori_loop(0, tokens // TOKENS_AT_ONCE, adjust, 0)
    for j in range(pair * SUBLANES):
        cols = slice(j * LANES, (j + 1) * LANES)
        gate = gate_ref[:, cols].astype(jnp.float32)
        value = mixed[j // SUBLANES, pl.ds(j % SUBLANES, tokens, stride=SUBLANES), :]
        value = value + skip_ref[:, cols] * act_ref[:, cols].astype(jnp.float32)
        out_ref[:, cols] = (value * (gate / (1.0 + jnp.exp(-gate)))).astype(jnp.bfloat16)


def finish(count, bc, y, cum, rates, everything, act, gate, skip):
    tokens, channels = act.shape
    blocks, state_count = rates.shape[:2]
    rows = tokens * SUBLANES
    pair = 2 if blocks % 2 == 0 else 1
    width = pair * GROUP
    peers, _, packed, _ = everything.shape
    return pl.pallas_call(
        functools.partial(finish_kernel, state_count),
        grid=(blocks // pair,),
        in_specs=[
            pl.BlockSpec(memory_space=pltpu.SMEM),
            pl.BlockSpec(memory_space=pltpu.SMEM),
            pl.BlockSpec((pair, rows, LANES), lambda i: (i, 0, 0)),
            pl.BlockSpec((pair, rows, LANES), lambda i: (i, 0, 0)),
            pl.BlockSpec((pair, state_count, SUBLANES, LANES), lambda i: (i, 0, 0, 0)),
            pl.BlockSpec((peers, pair, packed, LANES), lambda i: (0, i, 0, 0)),
            pl.BlockSpec((tokens, width), lambda i: (0, i)),
            pl.BlockSpec((tokens, width), lambda i: (0, i)),
            pl.BlockSpec((1, width), lambda i: (0, i)),
        ],
        out_specs=pl.BlockSpec((tokens, width), lambda i: (0, i)),
        out_shape=jax.ShapeDtypeStruct((tokens, channels), jnp.bfloat16),
        scratch_shapes=[
            pltpu.VMEM((pair, rows, LANES), jnp.float32),
            pltpu.VMEM((pair, state_count, SUBLANES, LANES), jnp.float32),
        ],
        compiler_params=params(),
        cost_estimate=pl.CostEstimate(
            flops=6 * tokens * channels * state_count,
            bytes_accessed=14 * tokens * channels,
            transcendentals=tokens * channels * state_count,
        ),
        name="carry_and_gate",
    )(count, bc, y, cum, rates, everything, act, gate, skip)


def attention_kernel(span, position, q_ref, *refs):
    key_refs = refs[: 1 + span]
    value_refs = refs[1 + span : 2 + 2 * span]
    out_ref, keys, values, scores = refs[2 + 2 * span :]
    tokens = q_ref.shape[0]

    @pl.when(pl.program_id(1) == 0)
    def _():
        first = lax.broadcasted_iota(jnp.int32, (tokens, HD), 1) == 0
        for d in range(span + 1):
            rows = slice(d * tokens, (d + 1) * tokens)
            absent = jnp.where(position[0] >= d, 0.0, FAR)
            keys[rows, :HD] = key_refs[d][0]
            keys[rows, HD:] = jnp.where(first, absent, 0.0).astype(jnp.bfloat16)
            values[rows, :HD] = value_refs[d][0]
            values[rows, HD:] = jnp.ones((tokens, HD), jnp.bfloat16)

    ones = (lax.broadcasted_iota(jnp.int32, (tokens, HD), 1) == 0).astype(jnp.bfloat16)
    query = jnp.concatenate([q_ref[...], ones], axis=1)
    near = lax.broadcasted_iota(jnp.int32, (tokens, tokens), 1) <= lax.broadcasted_iota(
        jnp.int32, (tokens, tokens), 0
    )

    def score(d):
        return lax.dot_general(
            query,
            keys[d * tokens : (d + 1) * tokens],
            (((1,), (1,)), ((), ())),
            preferred_element_type=jnp.float32,
        )

    block = jnp.where(near, score(0), score(span))
    scores[0] = block
    peak = block
    for d in range(1, span):
        block = score(d)
        scores[d] = block
        peak = jnp.maximum(peak, block)
    factor = LOG2E / math.sqrt(HD)
    peak = jnp.max(peak, axis=-1, keepdims=True) * factor
    weight = jnp.exp2(scores[0] * factor - peak).astype(jnp.bfloat16)
    zero = jnp.zeros_like(weight)
    total = jnp.dot(
        jnp.where(near, weight, zero), values[:tokens], preferred_element_type=jnp.float32
    ) + jnp.dot(
        jnp.where(near, zero, weight), values[span * tokens :], preferred_element_type=jnp.float32
    )
    for d in range(1, span):
        weight = jnp.exp2(scores[d] * factor - peak).astype(jnp.bfloat16)
        total = total + jnp.dot(
            weight, values[d * tokens : (d + 1) * tokens], preferred_element_type=jnp.float32
        )
    out_ref[...] = (total[:, :HD] / total[:, HD:]).astype(jnp.bfloat16)


def attention(position, queries, pairs, span):
    tokens, width = queries.shape
    kv_here = pairs.shape[2] // (2 * HD)
    grouping = width // HD // kv_here
    keys = tokens * (span + 1)

    def block(distance, offset):
        return pl.BlockSpec(
            (1, tokens, HD),
            lambda h, i, at: (jnp.maximum(at[0] - distance, 0), 0, offset + h),
        )

    specs = [pl.BlockSpec((tokens, HD), lambda h, i, at: (0, h * grouping + i))]
    specs += [block(d, 0) for d in range(span + 1)]
    specs += [block(d, kv_here) for d in range(span + 1)]
    return pl.pallas_call(
        functools.partial(attention_kernel, span),
        grid_spec=pltpu.PrefetchScalarGridSpec(
            num_scalar_prefetch=1,
            grid=(kv_here, grouping),
            in_specs=specs,
            out_specs=pl.BlockSpec((tokens, HD), lambda h, i, at: (0, h * grouping + i)),
            scratch_shapes=[
                pltpu.VMEM((keys, 2 * HD), jnp.bfloat16),
                pltpu.VMEM((keys, 2 * HD), jnp.bfloat16),
                pltpu.VMEM((span, tokens, tokens), jnp.float32),
            ],
        ),
        out_shape=jax.ShapeDtypeStruct((tokens, width), jnp.bfloat16),
        compiler_params=params(),
        cost_estimate=pl.CostEstimate(
            flops=8 * width * tokens * keys,
            bytes_accessed=4 * tokens * width + 4 * keys * HD * kv_here,
            transcendentals=width // HD * tokens * keys,
        ),
        name="window_attention",
    )(position, queries, *([pairs] * (2 * span + 2)))


def per_device(
    conv_in,
    gate_in,
    q_proj,
    k_proj,
    v_proj,
    conv_weight,
    conv_bias,
    proj_dt_weight,
    proj_bc_weight,
    dt_gain,
    dt_weight,
    dt_bias,
    decay_rate,
    skip_weight,
):
    tokens, channels = conv_in.shape
    span = WINDOW // tokens
    rank = dt_gain.shape[0]
    state_count = decay_rate.shape[0]
    blocks = channels // GROUP

    tail = shifted(conv_in[tokens - (KCONV - 1) :], "seq", 1)
    tail = jnp.pad(tail, ((TAIL - (KCONV - 1), 0), (0, 0)))
    pairs = lax.all_gather(jnp.concatenate([k_proj, v_proj], axis=1), "seq")
    position = lax.axis_index("seq").astype(jnp.int32).reshape(1)

    act, sums = project(
        tail, conv_in, conv_weight, conv_bias[None], proj_dt_weight, proj_bc_weight
    )
    if lax.axis_size("tp") == 2:
        sums = sums + lax.ppermute(sums, "tp", [(0, 1), (1, 0)])
    else:
        sums = lax.psum(sums, "tp")
    bc = sums[:, rank : rank + 2 * state_count].reshape(-1)
    rates = (
        (decay_rate * -LOG2E).reshape(state_count, blocks, SUBLANES, LANES).transpose(1, 0, 2, 3)
    )
    y, cum, packed = local_scan(bc, sums, dt_gain[None], dt_weight, dt_bias[None], act, rates)
    joined = join(rates, shifted(packed, "seq", 2), shifted(packed, "seq", 1))
    seq = lax.axis_size("seq")
    everything = lax.all_gather(
        joined, "seq", axis_index_groups=[list(range(0, seq, 2)), list(range(1, seq, 2))]
    )
    attn_at, _ = lax.optimization_barrier((position, joined))
    attn_out = attention(attn_at, q_proj, pairs, span)
    finish_at, attn_out = lax.optimization_barrier((position // 2 + 1, attn_out))
    mamba_out = finish(
        finish_at, bc, y, cum, rates, everything, act, gate_in, skip_weight[None]
    )
    return (mamba_out, attn_out)


def solution(mesh):
    return jax.shard_map(
        per_device,
        mesh=mesh,
        in_specs=(
            P("seq", "tp"),
            P("seq", "tp"),
            P("seq", "tp"),
            P("seq", "tp"),
            P("seq", "tp"),
            P(None, "tp"),
            P("tp"),
            P("tp", None),
            P(None, "tp"),
            P(),
            P(None, "tp"),
            P("tp"),
            P(None, "tp"),
            P("tp"),
        ),
        out_specs=(P("seq", "tp"), P("seq", "tp")),
        check_vma=False,
    )
```
